1024 devices in a mesh: group: 16 (over z, core), ingroup: 64 (over y, x).
Axes of the slice: x: 8, y: 8, z: 8, core: 2. Of those that a mesh axis runs over, the one named last changes fastest.
Arguments:
- tokens: bfloat16 [8192, 3584], P(('group', 'ingroup')), may hold values from -6 to 6
- gate_weight: bfloat16 [1024, 448, 1024], P(('group', 'ingroup')), may hold values from -0.09375 to 0.09375
- up_weight: bfloat16 [1024, 448, 1024], P(('group', 'ingroup')), may hold values from -0.09375 to 0.09375
- hidden_grad: bfloat16 [1024, 512, 128], P(('group', 'ingroup')), may hold values from -6 to 6
- expert_ids: int32 [8192, 8], P(('group', 'ingroup')), may hold values from 0 to 127, as said below
- expert_slot: int32 [8192, 8], P(('group', 'ingroup')), may hold values from -1 to 7, as said below
Outputs:
- token_grad: bfloat16 [8192, 3584], P(('group', 'ingroup'))
The draws below stay inside these ranges and needn't reach their ends.
Inputs may be any that keep to these rules, and one draw needn't show every extreme that they name: `expert_ids`: each row names 8 different experts that lie in exactly 4 different groups, the group of expert e being e // 8. `expert_slot`: entry (t, k) is -1 where token t is not among the first 4 tokens of its device, in token order, that name the group of expert_ids[t, k]. Among the other pairs that name one expert from the tokens of one column (all devices with one ingroup index, in token order), the first 8 get 0, 1, 2 and so on, and the rest -1.
All inputs are finite; a program needn't handle non-finite values.
Results may differ from the reference program's by a relative error of at most 0.0063.
Values may be sent and summed in bfloat16 or wider, within the bound.
A program may use at most 32 MiB of HBM per device.

```python
import jax
import jax.numpy as jnp
from jax import lax

D = 3584
HID = 1024
EXP_GRP = 8
TOPK = 8
GSEL = 4
TOK_DEV = 8
SHARDS = 8
DQ = 448
HQ = 128
EXPERTS = 128
ITEMS_OVERALL = 8192
CAP1 = 4
CAP2 = 8
CAP = 512
N_GROUP = 16
N_INGROUP = 64


def route_tables(key):
    key_groups, key_hot, key_experts = jax.random.split(key, 3)
    group_iota = jnp.arange(N_GROUP, dtype=jnp.int32)
    shard_tally = jnp.arange(EXP_GRP, dtype=jnp.int32)
    raw_groups = jax.random.randint(key_groups, (ITEMS_OVERALL, N_GROUP), 0, 65536, dtype=jnp.int32)
    group_scores = raw_groups * N_GROUP + group_iota[None, :]
    picked = lax.top_k(group_scores, GSEL)[1].astype(jnp.int32)
    hot_table = (jax.random.randint(key_hot, (N_GROUP * EXP_GRP,), 0, 8, dtype=jnp.int32) == 0).astype(jnp.int32) * 32768
    candidates = picked[:, :, None] * EXP_GRP + shard_tally[None, None, :]
    start_position_shift = jax.random.randint(key_experts, (ITEMS_OVERALL, GSEL, EXP_GRP), 0, 32768, dtype=jnp.int32) + hot_table[candidates]
    ranked = start_position_shift * EXP_GRP + shard_tally[None, None, :]
    strongest_specialist = lax.top_k(ranked, 1)[1].astype(jnp.int32)
    extra_preference = (shard_tally[None, None, :] == strongest_specialist).astype(jnp.int32) * 131072
    entire_feature_span = GSEL * EXP_GRP
    linear_tally = jnp.arange(entire_feature_span, dtype=jnp.int32).reshape(1, GSEL, EXP_GRP)
    dispatch_affinities = ((start_position_shift + extra_preference) * entire_feature_span + linear_tally).reshape(ITEMS_OVERALL, entire_feature_span)
    top_index = lax.top_k(dispatch_affinities, TOPK)[1].astype(jnp.int32)
    expert_ids = jnp.take_along_axis(candidates.reshape(ITEMS_OVERALL, entire_feature_span), top_index, axis=1).astype(jnp.int32)
    chosen = jnp.any((expert_ids // EXP_GRP)[:, :, None] == group_iota[None, None, :], axis=1)
    chosen_count = chosen.astype(jnp.int32).reshape(ITEMS_OVERALL // TOK_DEV, TOK_DEV, N_GROUP)
    rank = jnp.cumsum(chosen_count, axis=1) - 1
    group_slot = jnp.where((chosen_count > 0) & (rank < CAP1), rank, -1).reshape(ITEMS_OVERALL, N_GROUP).astype(jnp.int32)
    admitted = jnp.take_along_axis(group_slot, (expert_ids // EXP_GRP).astype(jnp.int32), axis=1) >= 0
    experts_count = N_GROUP * EXP_GRP
    expert_iota = jnp.arange(experts_count, dtype=jnp.int32)
    requests = jnp.sum(((expert_ids[:, :, None] == expert_iota[None, None, :]) & admitted[:, :, None]).astype(jnp.int32), axis=1)
    by_column = requests.reshape(N_GROUP, N_INGROUP, TOK_DEV, experts_count).transpose(1, 0, 2, 3)
    by_column = by_column.reshape(N_INGROUP, N_GROUP * TOK_DEV, experts_count)
    order = jnp.cumsum(by_column, axis=1) - 1
    order = order.reshape(N_INGROUP, N_GROUP, TOK_DEV, experts_count).transpose(1, 0, 2, 3).reshape(ITEMS_OVERALL, experts_count)
    slot_table = jnp.where((requests > 0) & (order < CAP2), order, -1).astype(jnp.int32)
    expert_slot = jnp.take_along_axis(slot_table, expert_ids, axis=1).astype(jnp.int32)
    return (expert_ids, expert_slot)


def draw_expert_ids(key, part):
    tables = route_tables(key)
    return tables[0]


def draw_expert_slot(key, part):
    tables = route_tables(key)
    return tables[1]


def steps_of(own_key, shape, cuts, least, high):
    gain = 1.0
    for dim, parts in cuts:
        steps = jax.random.uniform(jax.random.fold_in(jax.random.fold_in(own_key, 6), dim), (parts,), jnp.float32, least / len(cuts), high / len(cuts))
        gain = gain * jnp.repeat(jnp.exp(steps), shape[dim] // parts).reshape((-1,) + (1,) * (len(shape) - 1 - dim))
    return gain


def centred(key, extent, width, most, cuts=(), kind=jnp.bfloat16):
    factor_of = steps_of(key, extent, cuts, -0.22, 0.18) if cuts else 1.0
    result = jax.random.normal(key, extent, jnp.float32) * width * factor_of
    return jnp.minimum(jnp.maximum(result, -most), most).astype(kind)


def setup_inputs(seed: int = 0) -> dict:
    keys = jax.random.split(jax.random.key(seed), 7)
    tokens = centred(keys[0], (ITEMS_OVERALL, D), 1.0, 6.0, ((0, 1024),))
    gate_weight = centred(keys[1], (EXPERTS * SHARDS, DQ, HID), D ** -0.5, 0.09375, ((0, 1024),))
    up_weight = centred(keys[2], (EXPERTS * SHARDS, DQ, HID), D ** -0.5, 0.09375, ((0, 1024),))
    hidden_grad = centred(keys[3], (EXPERTS * SHARDS, CAP, HQ), 1.0, 6.0, ((0, 1024),))
    expert_ids = draw_expert_ids(jax.random.fold_in(keys[6], 71), 0)
    expert_slot = draw_expert_slot(jax.random.fold_in(keys[6], 71), 0)
    return {"tokens": tokens, "gate_weight": gate_weight, "up_weight": up_weight, "hidden_grad": hidden_grad, "expert_ids": expert_ids, "expert_slot": expert_slot}


def activation_grads(pre_gate, pre_up, hidden):
    sigmoid_gate = jax.nn.sigmoid(pre_gate)
    gate_grad = (hidden * pre_up * sigmoid_gate * (1.0 + pre_gate * (1.0 - sigmoid_gate))).astype(jnp.bfloat16)
    up_grad = (hidden * pre_gate * sigmoid_gate).astype(jnp.bfloat16)
    return gate_grad, up_grad


def reference(tokens, gate_weight, up_weight, hidden_grad, expert_ids, expert_slot):
    gate_all = gate_weight.reshape(EXPERTS, D, HID)
    up_all = up_weight.reshape(EXPERTS, D, HID)
    hidden_all = hidden_grad.reshape(EXPERTS, SHARDS, CAP, HQ).transpose(0, 2, 1, 3).reshape(EXPERTS, CAP, HID)
    token_index = jnp.arange(ITEMS_OVERALL, dtype=jnp.int32)
    column = ((token_index // TOK_DEV) % N_INGROUP).astype(jnp.int32)
    group_of = (expert_ids // EXP_GRP).astype(jnp.int32)
    group_iota = jnp.arange(N_GROUP, dtype=jnp.int32)
    chosen = jnp.any(group_of[:, :, None] == group_iota[None, None, :], axis=1).astype(jnp.int32)
    chosen_blocks = chosen.reshape(ITEMS_OVERALL // TOK_DEV, TOK_DEV, N_GROUP)
    rank = jnp.cumsum(chosen_blocks, axis=1) - 1
    group_slot = jnp.where((chosen_blocks > 0) & (rank < CAP1), rank, -1).reshape(ITEMS_OVERALL, N_GROUP).astype(jnp.int32)
    admitted = (jnp.take_along_axis(group_slot, group_of, axis=1) >= 0) & (expert_slot >= 0)
    flat_slot = jnp.where(admitted, expert_ids * CAP + column[:, None] * CAP2 + expert_slot, EXPERTS * CAP).astype(jnp.int32)
    owners = jnp.full((EXPERTS * CAP + 1,), ITEMS_OVERALL, jnp.int32)
    owner_values = jnp.broadcast_to(token_index[:, None], (ITEMS_OVERALL, TOPK)).reshape(-1).astype(jnp.int32)
    owners = owners.at[flat_slot.reshape(-1)].set(owner_values)
    owners = owners[: EXPERTS * CAP].reshape(EXPERTS, CAP)
    padded = jnp.concatenate([tokens, jnp.zeros((1, D), tokens.dtype)], axis=0)
    highest = lax.Precision.HIGHEST

    def one_expert(pieces):
        gate_expert, up_expert, hidden_expert, owner_expert = pieces
        slot_rows = padded[owner_expert].astype(jnp.float32)
        gate_float = gate_expert.astype(jnp.float32)
        up_float = up_expert.astype(jnp.float32)
        pre_gate = jnp.dot(slot_rows, gate_float, precision=highest)
        pre_up = jnp.dot(slot_rows, up_float, precision=highest)
        gate_grad, up_grad = activation_grads(pre_gate, pre_up, hidden_expert.astype(jnp.float32))
        returned_rows = jnp.dot(gate_grad.astype(jnp.float32), gate_float.T, precision=highest)
        returned_rows = returned_rows + jnp.dot(up_grad.astype(jnp.float32), up_float.T, precision=highest)
        return returned_rows.astype(jnp.bfloat16)

    slot_grad = lax.map(one_expert, (gate_all, up_all, hidden_all, owners)).reshape(EXPERTS * CAP, D)
    safe_slot = jnp.where(admitted, flat_slot, 0).astype(jnp.int32)
    running = jnp.zeros((ITEMS_OVERALL, D), jnp.float32)
    for group_index in range(N_GROUP):
        partial_sum = jnp.zeros((ITEMS_OVERALL, D), jnp.float32)
        for chosen_index in range(TOPK):
            usable = admitted[:, chosen_index] & (group_of[:, chosen_index] == group_index)
            partial_sum = partial_sum + jnp.where(usable[:, None], slot_grad[safe_slot[:, chosen_index]].astype(jnp.float32), 0.0)
        rounded = lax.optimization_barrier(partial_sum.astype(jnp.bfloat16))
        running = running + rounded.astype(jnp.float32)
    return running.astype(jnp.bfloat16)
```

```python
import functools

import jax
import jax.numpy as jnp
from jax import lax
from jax.experimental import pallas as pl
from jax.experimental.pallas import tpu as pltpu
from jax.sharding import PartitionSpec as P

MESH = pl.DeviceIdType.MESH
BF = jnp.bfloat16
F32 = jnp.float32
CORES = 2
EXP_GRP = 8
CAP1 = 4
CAP2 = 8
META = 64
VMEM_BYTES = 48 * 1024 * 1024


def remote(src, dst, send_sem, recv_sem, device):
    return pltpu.make_async_remote_copy(
        src_ref=src,
        dst_ref=dst,
        send_sem=send_sem,
        recv_sem=recv_sem,
        device_id=device,
        device_id_type=MESH,
    )


def offsets(n):
    order = [0]
    for k in range(1, n // 2):
        order += [k, -k]
    return order + [n // 2]


def dot_nt(a, b):
    return lax.dot_general(a, b, (((1,), (1,)), ((), ())), preferred_element_type=F32)


def dot_tn(a, b):
    return lax.dot_general(a, b, (((0,), (0,)), ((), ())), preferred_element_type=F32)


def kernel(
    dims,
    tok,
    wg,
    wu,
    hg,
    out,
    a_buf,
    g_buf,
    s_buf,
    r_buf,
    w2,
    h_buf,
    rs_s,
    rs_r,
    ag,
    acc,
    t_buf,
    u_buf,
    sel_buf,
    gp,
    cx,
    q_buf,
    zb,
    o_buf,
    f_buf,
    w_sem,
    h_sem,
    x1,
    z1,
    c1,
    y1,
    rs_sem,
    ag_sem,
    y2,
    c2,
    z2,
    x2,
):
    NX, NY, NZ = dims
    NG = NZ * CORES
    TD = tok.shape[1]
    DQ = r_buf.shape[3]
    HQ = hg.shape[1]
    LANES = tok.shape[2]
    RG = NX * CAP2
    MC = 2 * RG
    NCH = NY // 2
    half_x = NX // 2
    order = offsets(NY)

    g = lax.axis_index("group")
    p = lax.axis_index("ingroup")
    z, c = lax.div(g, CORES), lax.rem(g, CORES)
    y, x = lax.div(p, NX), lax.rem(p, NX)

    def xat(o):
        return lax.rem(x + (o + NX), NX)

    def yat(o):
        return lax.rem(y + (o + NY), NY)

    def zat(o):
        return lax.rem(z + (o + NZ), NZ)

    def at_x(xx):
        return (g, y * NX + xx)

    def at_y(yy):
        return (g, yy * NX + x)

    def at_z(zz):
        return (zz * CORES + c, p)

    sibling = (z * CORES + (1 - c), p)

    sends = []

    def start(copy):
        copy.start()
        sends.append(copy)

    loads = []
    for d in range(NX):
        for n, w in enumerate((wg, wu)):
            loads.append(
                pltpu.make_async_copy(
                    w.at[:, pl.ds(d * HQ, HQ)],
                    w2.at[d, :, pl.ds(n * HQ, HQ)],
                    w_sem.at[d * 2 + n],
                )
            )
    loads.append(pltpu.make_async_copy(hg, h_buf, h_sem.at[0]))
    for load in loads:
        load.start()

    barrier = pltpu.get_barrier_semaphore()
    peers = [at_x(xat(o)) for o in range(1, NX)]
    peers += [at_y(yat(o)) for o in range(1, NY)]
    peers += [at_z(zat(o)) for o in range(1, NZ)]
    peers += [sibling]
    for peer in peers:
        pl.semaphore_signal(barrier, inc=1, device_id=peer, device_id_type=MESH)
    pl.semaphore_wait(barrier, len(peers))

    for o in range(1, NX):
        xd = xat(o)
        start(remote(tok.at[xd], a_buf.at[x], x1.at[0, o], x1.at[1, o], at_x(xd)))
    a_buf[pl.ds(x, 1)] = tok[pl.ds(x, 1)]
    for o in range(1, NX):
        xs = xat(-o)
        remote(tok.at[xs], a_buf.at[xs], x1.at[0, o], x1.at[1, o], at_x(xs)).wait_recv()

    for o in range(1, NZ):
        zd = zat(o)
        start(remote(a_buf, g_buf.at[:, g], z1.at[0, o], z1.at[1, o], at_z(zd)))
    start(remote(a_buf, g_buf.at[:, g], c1.at[0, 0], c1.at[1, 0], sibling))
    g_buf[:, pl.ds(g, 1)] = a_buf[...].reshape(NX, 1, TD, LANES)
    for o in range(1, NZ):
        gs = zat(-o) * CORES + c
        remote(a_buf, g_buf.at[:, gs], z1.at[0, o], z1.at[1, o], at_z(zat(-o))).wait_recv()
        start(remote(g_buf.at[:, gs], g_buf.at[:, gs], c1.at[0, o], c1.at[1, o], sibling))
    for o in range(NZ):
        gs = zat(-o) * CORES + (1 - c)
        remote(a_buf, g_buf.at[:, gs], c1.at[0, o], c1.at[1, o], sibling).wait_recv()

    pick_row = lax.broadcasted_iota(jnp.int32, (8, 128), 0)
    pick_lane = lax.broadcasted_iota(jnp.int32, (8, 128), 1)
    pick = jnp.where(pick_lane == 64 + pick_row, 8.0, jnp.where(pick_lane == 72 + pick_row, 1.0, 0.0))
    pick = pick.astype(BF)
    code_of = lax.broadcasted_iota(jnp.int32, (NY * CAP2, NG * TD), 0) + g * (NY * CAP2)
    code_of = code_of.astype(F32)
    for xc in range(NX):
        rows = g_buf[xc].reshape(NG * TD, LANES)
        codes = dot_nt(pick, rows[:, LANES - 128 :])
        sel = jnp.zeros(code_of.shape, F32)
        for k in range(8):
            sel = jnp.where(codes[k : k + 1, :] == code_of, 1.0, sel)
        sel = sel.astype(BF)
        sel_buf[xc] = sel
        picked = jnp.dot(sel, rows[:, :DQ], preferred_element_type=F32).astype(BF)
        s_buf[:, xc] = picked.reshape(NY, CAP2, DQ)

    for i in range(1, NY):
        yd = yat(-order[i])
        start(remote(s_buf.at[yd], r_buf.at[i], y1.at[0, i], y1.at[1, i], at_y(yd)))
    r_buf[pl.ds(0, 1)] = s_buf[pl.ds(y, 1)]
    for load in loads:
        load.wait()

    def weights(d):
        return w2[pl.ds(d, 1)].reshape(DQ, 2 * HQ)

    def slot_rows(j):
        return r_buf[2 * j : 2 * j + 2].reshape(MC, DQ)

    def rs_copy(way, k, j):
        rows = pl.ds(j * MC, MC) if k else pl.ds(j * MC + way * RG, RG)
        sign = 1 - 2 * way
        return remote(
            rs_s.at[way, k, rows],
            rs_r.at[way, k, rows],
            rs_sem.at[0, way, k, j],
            rs_sem.at[1, way, k, j],
            at_x(xat(sign)),
        )

    def ag_copy(way, k, j, src):
        rows = pl.ds(j * MC, MC) if k < half_x - 1 else pl.ds(j * MC + way * RG, RG)
        sign = 1 - 2 * way
        return remote(
            ag.at[src, rows],
            ag.at[src, rows],
            ag_sem.at[0, way, k, j],
            ag_sem.at[1, way, k, j],
            at_x(xat(sign)),
        )

    def y_back(i):
        yd = yat(order[i])
        return remote(t_buf.at[i], u_buf.at[y], y2.at[0, i], y2.at[1, i], at_y(yd))

    def rs_stage(k, j):
        if k == 0:
            for i in (2 * j, 2 * j + 1):
                if i:
                    ys = yat(order[i])
                    remote(s_buf.at[ys], r_buf.at[i], y1.at[0, i], y1.at[1, i], at_y(ys)).wait_recv()
        base = j * MC
        lhs = slot_rows(j)
        for way in range(2):
            sign = 1 - 2 * way
            w = weights(xat(sign * (half_x - k)))
            mine = pl.ds(base + way * RG, RG)
            other = pl.ds(base + (1 - way) * RG, RG)
            if k == 0:
                part = lhs[way * RG : way * RG + RG]
                rs_s[way, 0, mine] = jnp.dot(part, w, preferred_element_type=F32).astype(BF)
            else:
                part = jnp.dot(lhs, w, preferred_element_type=F32)
                rs_copy(way, k - 1, j).wait_recv()
                if k == 1:
                    own = part[way * RG : way * RG + RG]
                    rest = part[(1 - way) * RG : (1 - way) * RG + RG]
                    rs_s[way, 1, mine] = (own + rs_r[way, 0, mine].astype(F32)).astype(BF)
                    rs_s[way, 1, other] = rest.astype(BF)
                else:
                    rows = pl.ds(base, MC)
                    rs_s[way, k, rows] = (part + rs_r[way, k - 1, rows].astype(F32)).astype(BF)
            start(rs_copy(way, k, j))

    def act_stage(j):
        rows = pl.ds(j * MC, MC)
        pre = jnp.dot(slot_rows(j), weights(x), preferred_element_type=F32)
        for way in range(2):
            rs_copy(way, half_x - 1, j).wait_recv()
            pre = pre + rs_r[way, half_x - 1, rows].astype(F32)
        pre_gate, pre_up = pre[:, :HQ], pre[:, HQ:]
        hidden = jnp.concatenate(
            [
                h_buf[pl.ds(yat(order[i]) * RG, RG)].astype(F32)
                for i in (2 * j, 2 * j + 1)
            ],
            axis=0,
        )
        sig = jax.nn.sigmoid(pre_gate)
        both = jnp.concatenate(
            [
                (hidden * pre_up * sig * (1.0 + pre_gate * (1.0 - sig))).astype(BF),
                (hidden * pre_gate * sig).astype(BF),
            ],
            axis=1,
        )
        ag[pl.ds(x, 1), rows] = both.reshape(1, MC, 2 * HQ)
        for way in range(2):
            start(ag_copy(way, 0, j, x))
        acc[rows] = dot_nt(both, weights(x))

    def ag_stage(k, j):
        rows = pl.ds(j * MC, MC)
        for way in range(2):
            sign = 1 - 2 * way
            src = xat(-sign * k)
            ag_copy(way, k - 1, j, src).wait_recv()
            if k < half_x:
                start(ag_copy(way, k, j, src))
        if k < half_x:
            total = acc[rows]
            for src in (xat(-k), xat(k)):
                block = ag[pl.ds(src, 1), rows].reshape(MC, 2 * HQ)
                total = total + dot_nt(block, weights(src))
            acc[rows] = total
        else:
            src = xat(half_x)
            block = ag[pl.ds(src, 1), rows].reshape(MC, 2 * HQ)
            total = acc[rows] + dot_nt(block, weights(src))
            t_buf[2 * j : 2 * j + 2] = total.astype(BF).reshape(2, NX, CAP2, DQ)
            for i in (2 * j, 2 * j + 1):
                if i:
                    start(y_back(i))

    stages = [functools.partial(rs_stage, k) for k in range(half_x)]
    stages += [act_stage]
    stages += [functools.partial(ag_stage, k) for k in range(1, half_x + 1)]
    for t in range(len(stages) + NCH - 1):
        for j in range(NCH):
            if 0 <= t - j < len(stages):
                stages[t - j](j)

    u_buf[pl.ds(y, 1)] = t_buf[pl.ds(0, 1)]
    for i in range(1, NY):
        ys = yat(-order[i])
        remote(t_buf.at[i], u_buf.at[ys], y2.at[0, i], y2.at[1, i], at_y(ys)).wait_recv()
    for xc in range(NX):
        rows = u_buf[:, xc].reshape(NY * CAP2, DQ)
        sums = dot_tn(sel_buf[xc], rows).astype(BF)
        gp[:, :, xc] = sums.reshape(NZ, CORES, TD, DQ)

    pair = remote(gp.at[:, 1 - c], cx, c2.at[0], c2.at[1], sibling)
    start(pair)
    pair.wait_recv()
    for o in range(1, NZ):
        zd = zat(o)
        mine = gp[pl.ds(zd, 1), pl.ds(c, 1)].reshape(1, NX, TD, DQ).astype(F32)
        q_buf[pl.ds(o, 1)] = (mine + cx[pl.ds(zd, 1)].astype(F32)).astype(BF)
        start(remote(q_buf.at[o], zb.at[o], z2.at[0, o], z2.at[1, o], at_z(zd)))
    total = gp[pl.ds(z, 1), pl.ds(c, 1)].reshape(1, NX, TD, DQ).astype(F32)
    total = total + cx[pl.ds(z, 1)].astype(F32)
    for o in range(1, NZ):
        remote(q_buf.at[o], zb.at[o], z2.at[0, o], z2.at[1, o], at_z(zat(-o))).wait_recv()
        total = total + zb[pl.ds(o, 1)].astype(F32)
    o_buf[...] = total.reshape(NX, TD, DQ).astype(BF)

    for o in range(1, NX):
        xd = xat(o)
        start(remote(o_buf.at[xd], f_buf.at[x], x2.at[0, o], x2.at[1, o], at_x(xd)))
    f_buf[pl.ds(x, 1)] = o_buf[pl.ds(x, 1)]
    for o in range(1, NX):
        xs = xat(-o)
        remote(o_buf.at[xs], f_buf.at[xs], x2.at[0, o], x2.at[1, o], at_x(xs)).wait_recv()
    out[...] = f_buf[...]
    for copy in sends:
        copy.wait_send()


def routes(expert_ids, expert_slot, groups):
    group_of = expert_ids // EXP_GRP
    named = jnp.any(group_of[:, :, None] == jnp.arange(groups)[None, None, :], axis=1)
    rank = jnp.cumsum(named.astype(jnp.int32), axis=0) - 1
    fits = named & (rank < CAP1)
    in_group = jnp.any(
        fits[:, None, :] & (group_of[:, :, None] == jnp.arange(groups)[None, None, :]), axis=2
    )
    admitted = in_group & (expert_slot >= 0)
    names = jnp.where(admitted, expert_ids, 255)
    slots = jnp.where(admitted, expert_slot, 0)
    rest = jnp.zeros((expert_ids.shape[0], META - 16), jnp.int32)
    return jnp.concatenate([names, slots, rest], axis=1).astype(BF)


def shards(tokens, gate_weight, up_weight, hidden_grad, expert_ids, expert_slot):
    NG = lax.axis_size("group")
    NY = EXP_GRP
    NX = lax.axis_size("ingroup") // NY
    NZ = NG // CORES
    TD, D = tokens.shape
    DQ = D // NX
    HQ = hidden_grad.shape[2]
    CAP = hidden_grad.shape[1]
    LANES = DQ + META
    meta = routes(expert_ids, expert_slot, NG)
    blocks = tokens.reshape(TD, NX, DQ).transpose(1, 0, 2)
    blocks = jnp.concatenate([blocks, jnp.broadcast_to(meta[None], (NX, TD, META))], axis=2)
    half_x = NX // 2
    NCH = NY // 2
    vmem = pl.BlockSpec(memory_space=pltpu.VMEM)
    hbm = pl.BlockSpec(memory_space=pl.ANY)
    dma = pltpu.SemaphoreType.DMA
    result = pl.pallas_call(
        functools.partial(kernel, (NX, NY, NZ)),
        out_shape=jax.ShapeDtypeStruct((NX, TD, DQ), BF),
        in_specs=[vmem, hbm, hbm, hbm],
        out_specs=vmem,
        scratch_shapes=[
            pltpu.VMEM((NX, TD, LANES), BF),
            pltpu.VMEM((NX, NG, TD, LANES), BF),
            pltpu.VMEM((NY, NX, CAP2, DQ), BF),
            pltpu.VMEM((NY, NX, CAP2, DQ), BF),
            pltpu.VMEM((NX, DQ, 2 * HQ), BF),
            pltpu.VMEM((CAP, HQ), BF),
            pltpu.VMEM((2, half_x, CAP, 2 * HQ), BF),
            pltpu.VMEM((2, half_x, CAP, 2 * HQ), BF),
            pltpu.VMEM((NX, CAP, 2 * HQ), BF),
            pltpu.VMEM((CAP, DQ), F32),
            pltpu.VMEM((NY, NX, CAP2, DQ), BF),
            pltpu.VMEM((NY, NX, CAP2, DQ), BF),
            pltpu.VMEM((NX, NY * CAP2, NG * TD), BF),
            pltpu.VMEM((NZ, CORES, NX, TD, DQ), BF),
            pltpu.VMEM((NZ, NX, TD, DQ), BF),
            pltpu.VMEM((NZ, NX, TD, DQ), BF),
            pltpu.VMEM((NZ, NX, TD, DQ), BF),
            pltpu.VMEM((NX, TD, DQ), BF),
            pltpu.VMEM((NX, TD, DQ), BF),
            dma((NX * 2,)),
            dma((1,)),
            dma((2, NX)),
            dma((2, NZ)),
            dma((2, NZ)),
            dma((2, NY)),
            dma((2, 2, half_x, NCH)),
            dma((2, 2, half_x, NCH)),
            dma((2, NY)),
            dma((2,)),
            dma((2, NZ)),
            dma((2, NX)),
        ],
        compiler_params=pltpu.CompilerParams(
            collective_id=0, has_side_effects=True, vmem_limit_bytes=VMEM_BYTES
        ),
    )(blocks, gate_weight[0], up_weight[0], hidden_grad[0])
    return result.transpose(1, 0, 2).reshape(TD, D)


def solution(mesh):
    in_specs = (
        P(("group", "ingroup"), None),
        P(("group", "ingroup"), None, None),
        P(("group", "ingroup"), None, None),
        P(("group", "ingroup"), None, None),
        P(("group", "ingroup"), None),
        P(("group", "ingroup"), None),
    )
    out_specs = P(("group", "ingroup"), None)
    return jax.shard_map(shards, mesh=mesh, in_specs=in_specs, out_specs=out_specs, check_vma=False)
```

```python
import functools

import jax
import jax.numpy as jnp
from jax import lax
from jax.experimental import pallas as pl
from jax.experimental.pallas import tpu as pltpu
from jax.sharding import PartitionSpec as P

MESH = pl.DeviceIdType.MESH
BF = jnp.bfloat16
F32 = jnp.float32
CORES = 2
EXP_GRP = 8
CAP1 = 4
CAP2 = 8
META = 64
CPC = 2
VMEM_BYTES = 48 * 1024 * 1024


def remote(src, dst, send_sem, recv_sem, device):
    return pltpu.make_async_remote_copy(
        src_ref=src,
        dst_ref=dst,
        send_sem=send_sem,
        recv_sem=recv_sem,
        device_id=device,
        device_id_type=MESH,
    )


def dot_nt(a, b):
    return lax.dot_general(a, b, (((1,), (1,)), ((), ())), preferred_element_type=F32)


def dot_tn(a, b):
    return lax.dot_general(a, b, (((0,), (0,)), ((), ())), preferred_element_type=F32)


def kernel(
    dims,
    tokens,
    ids,
    slots,
    wg,
    wu,
    hg,
    out,
    tok_in,
    ids_in,
    slots_in,
    tok,
    a_buf,
    g_buf,
    s_buf,
    r_buf,
    w2,
    h_buf,
    rs_s,
    rs_r,
    ag,
    acc,
    t_buf,
    u_buf,
    sel_buf,
    gp,
    cx,
    q_buf,
    zb,
    o_buf,
    f_buf,
    in_sem,
    w_sem,
    x1,
    z1,
    c1,
    y1,
    rs_sem,
    ag_sem,
    y2,
    c2,
    z2,
    x2,
):
    NX, NY, NZ = dims
    NG = NZ * CORES
    TD = tok.shape[1]
    LANES = tok.shape[2]
    DQ = LANES - META
    HQ = hg.shape[1]
    RG = NX * CAP2
    CR = CPC * CAP2
    MC = NY * CR
    HALF = MC // 2
    NCH = NX // CPC
    half_x = NX // 2

    g = lax.axis_index("group")
    p = lax.axis_index("ingroup")
    z, c = lax.div(g, CORES), lax.rem(g, CORES)
    y, x = lax.div(p, NX), lax.rem(p, NX)

    def xat(o):
        return lax.rem(x + (o + NX), NX)

    def yat(o):
        return lax.rem(y + (o + NY), NY)

    def zat(o):
        return lax.rem(z + (o + NZ), NZ)

    def at_x(xx):
        return (g, y * NX + xx)

    def at_y(yy):
        return (g, yy * NX + x)

    def at_z(zz):
        return (zz * CORES + c, p)

    sibling = (z * CORES + (1 - c), p)
    sends = []

    def start(copy):
        copy.start()
        sends.append(copy)

    inputs = [
        pltpu.make_async_copy(ids, ids_in, in_sem.at[0]),
        pltpu.make_async_copy(slots, slots_in, in_sem.at[1]),
        pltpu.make_async_copy(tokens, tok_in, in_sem.at[2]),
    ]
    for load in inputs:
        load.start()

    barrier = pltpu.get_barrier_semaphore()
    peers = [at_x(xat(o)) for o in range(1, NX)]
    peers += [at_y(yat(o)) for o in range(1, NY)]
    peers += [at_z(zat(o)) for o in range(1, NZ)]
    peers += [sibling]
    for peer in peers:
        pl.semaphore_signal(barrier, inc=1, device_id=peer, device_id_type=MESH)

    loads = []
    for d in range(NX):
        for n, w in enumerate((wg, wu)):
            loads.append(
                pltpu.make_async_copy(
                    w.at[:, pl.ds(d * HQ, HQ)],
                    w2.at[d, :, pl.ds(n * HQ, HQ)],
                    w_sem.at[d * 2 + n],
                )
            )
    loads.append(pltpu.make_async_copy(hg, h_buf, in_sem.at[3]))
    for load in loads:
        load.start()
    for load in inputs:
        load.wait()

    names, places = ids_in[...], slots_in[...]
    group_of = lax.div(names, EXP_GRP)
    lane = lax.broadcasted_iota(jnp.int32, (TD, 128), 1)
    named = jnp.zeros((TD, 128), F32)
    for k in range(names.shape[1]):
        named = jnp.where(group_of[:, k : k + 1] == lane, 1.0, named)
    before = lax.broadcasted_iota(jnp.int32, (TD, TD), 1) < lax.broadcasted_iota(jnp.int32, (TD, TD), 0)
    rank = jnp.dot(
        jnp.where(before, 1.0, 0.0).astype(BF), named.astype(BF), preferred_element_type=F32
    )
    fits = jnp.where(rank < CAP1, named, 0.0)
    meta = jnp.zeros((TD, 128), F32)
    for k in range(names.shape[1]):
        in_group = jnp.sum(jnp.where(group_of[:, k : k + 1] == lane, fits, 0.0), axis=1, keepdims=True)
        place = places[:, k : k + 1]
        name = jnp.where((in_group > 0.0) & (place >= 0), names[:, k : k + 1], 255).astype(F32)
        meta = jnp.where(lane == k, name, meta)
        meta = jnp.where(lane == 8 + k, jnp.maximum(place, 0).astype(F32), meta)
    features = tok_in[...].astype(F32)
    for d in range(NX):
        block = jnp.concatenate([features[:, d * DQ : (d + 1) * DQ], meta[:, :META]], axis=1)
        tok[d] = block.astype(BF)
    pl.semaphore_wait(barrier, len(peers))

    for o in range(1, NX):
        xd = xat(o)
        start(remote(tok.at[xd], a_buf.at[x], x1.at[0, o], x1.at[1, o], at_x(xd)))
    a_buf[pl.ds(x, 1)] = tok[pl.ds(x, 1)]
    for o in range(1, NX):
        xs = xat(-o)
        remote(tok.at[xs], a_buf.at[xs], x1.at[0, o], x1.at[1, o], at_x(xs)).wait_recv()

    def z_copy(o, j, src, dst):
        cols = pl.ds(j * CPC, CPC)
        return remote(
            a_buf.at[cols], g_buf.at[cols, src, c], z1.at[0, o, j], z1.at[1, o, j], at_z(dst)
        )

    for j in range(NCH):
        for o in range(1, NZ):
            start(z_copy(o, j, z, zat(o)))
    g_buf[:, pl.ds(z, 1), pl.ds(c, 1)] = a_buf[...].reshape(NX, 1, 1, TD, LANES)

    def core_copy(j, core):
        part = g_buf.at[pl.ds(j * CPC, CPC), :, core]
        return remote(part, part, c1.at[0, j], c1.at[1, j], sibling)

    def gather_stage(j):
        for o in range(1, NZ):
            z_copy(o, j, zat(-o), zat(-o)).wait_recv()
        start(core_copy(j, c))

    pick_row = lax.broadcasted_iota(jnp.int32, (8, 128), 0)
    pick_lane = lax.broadcasted_iota(jnp.int32, (8, 128), 1) - (128 - META)
    pick = jnp.where(pick_lane == pick_row, 8.0, jnp.where(pick_lane == 8 + pick_row, 1.0, 0.0))
    pick = pick.astype(BF)
    code_of = lax.broadcasted_iota(jnp.int32, (NY * CAP2, NG * TD), 0) + g * (NY * CAP2)
    code_of = code_of.astype(F32)

    def y_copy(o, j, src, dst):
        return remote(
            s_buf.at[j, dst], r_buf.at[j, src], y1.at[0, o, j], y1.at[1, o, j], at_y(dst)
        )

    def pick_stage(j):
        core_copy(j, 1 - c).wait_recv()
        for q in range(CPC):
            xc = j * CPC + q
            rows = g_buf[xc].reshape(NG * TD, LANES)
            codes = dot_nt(pick, rows[:, LANES - 128 :])
            sel = jnp.zeros(code_of.shape, F32)
            for k in range(8):
                sel = jnp.where(codes[k : k + 1, :] == code_of, 1.0, sel)
            sel = sel.astype(BF)
            sel_buf[xc] = sel
            picked = jnp.dot(sel, rows[:, :DQ], preferred_element_type=F32).astype(BF)
            s_buf[j, :, q] = picked.reshape(NY, CAP2, DQ)
        for o in range(1, NY):
            start(y_copy(o, j, y, yat(o)))
        r_buf[j, pl.ds(y, 1)] = s_buf[j, pl.ds(y, 1)]

    def weights(d):
        return w2[pl.ds(d, 1)].reshape(DQ, 2 * HQ)

    def slot_rows(j):
        return r_buf[j].reshape(MC, DQ)

    def rs_copy(way, k, j):
        rows = pl.ds(j * MC, MC) if k else pl.ds(j * MC + way * HALF, HALF)
        return remote(
            rs_s.at[way, k, rows],
            rs_r.at[way, k, rows],
            rs_sem.at[0, way, k, j],
            rs_sem.at[1, way, k, j],
            at_x(xat(1 - 2 * way)),
        )

    def ag_copy(way, k, j, src):
        rows = pl.ds(j * MC, MC) if k < half_x - 1 else pl.ds(j * MC + way * HALF, HALF)
        return remote(
            ag.at[src, rows],
            ag.at[src, rows],
            ag_sem.at[0, way, k, j],
            ag_sem.at[1, way, k, j],
            at_x(xat(1 - 2 * way)),
        )

    def rs_stage(k, j):
        if k == 0:
            for o in range(1, NY):
                y_copy(o, j, yat(-o), yat(-o)).wait_recv()
            if j == 0:
                for load in loads:
                    load.wait()
        base = j * MC
        lhs = slot_rows(j)
        for way in range(2):
            sign = 1 - 2 * way
            w = weights(xat(sign * (half_x - k)))
            mine = pl.ds(base + way * HALF, HALF)
            other = pl.ds(base + (1 - way) * HALF, HALF)
            if k == 0:
                part = lhs[way * HALF : way * HALF + HALF]
                rs_s[way, 0, mine] = jnp.dot(part, w, preferred_element_type=F32).astype(BF)
            else:
                part = jnp.dot(lhs, w, preferred_element_type=F32)
                rs_copy(way, k - 1, j).wait_recv()
                if k == 1:
                    own = part[way * HALF : way * HALF + HALF]
                    rest = part[(1 - way) * HALF : (1 - way) * HALF + HALF]
                    rs_s[way, 1, mine] = (own + rs_r[way, 0, mine].astype(F32)).astype(BF)
                    rs_s[way, 1, other] = rest.astype(BF)
                else:
                    rows = pl.ds(base, MC)
                    rs_s[way, k, rows] = (part + rs_r[way, k - 1, rows].astype(F32)).astype(BF)
            start(rs_copy(way, k, j))

    def act_stage(j):
        rows = pl.ds(j * MC, MC)
        pre = jnp.dot(slot_rows(j), weights(x), preferred_element_type=F32)
        for way in range(2):
            rs_copy(way, half_x - 1, j).wait_recv()
            pre = pre + rs_r[way, half_x - 1, rows].astype(F32)
        pre_gate, pre_up = pre[:, :HQ], pre[:, HQ:]
        hidden = jnp.concatenate(
            [h_buf[ys * RG + j * CR : ys * RG + (j + 1) * CR] for ys in range(NY)], axis=0
        ).astype(F32)
        sig = jax.nn.sigmoid(pre_gate)
        both = jnp.concatenate(
            [
                (hidden * pre_up * sig * (1.0 + pre_gate * (1.0 - sig))).astype(BF),
                (hidden * pre_gate * sig).astype(BF),
            ],
            axis=1,
        )
        ag[pl.ds(x, 1), rows] = both.reshape(1, MC, 2 * HQ)
        for way in range(2):
            start(ag_copy(way, 0, j, x))
        acc[rows] = dot_nt(both, weights(x))

    def back_copy(o, j, src, dst):
        return remote(
            t_buf.at[j, dst], u_buf.at[j, src], y2.at[0, o, j], y2.at[1, o, j], at_y(dst)
        )

    def ag_stage(k, j):
        rows = pl.ds(j * MC, MC)
        for way in range(2):
            sign = 1 - 2 * way
            src = xat(-sign * k)
            ag_copy(way, k - 1, j, src).wait_recv()
            if k < half_x:
                start(ag_copy(way, k, j, src))
        if k < half_x:
            total = acc[rows]
            for src in (xat(-k), xat(k)):
                block = ag[pl.ds(src, 1), rows].reshape(MC, 2 * HQ)
                total = total + dot_nt(block, weights(src))
            acc[rows] = total
        else:
            src = xat(half_x)
            block = ag[pl.ds(src, 1), rows].reshape(MC, 2 * HQ)
            total = acc[rows] + dot_nt(block, weights(src))
            t_buf[j] = total.astype(BF).reshape(NY, CPC, CAP2, DQ)
            for o in range(1, NY):
                start(back_copy(o, j, y, yat(o)))
            u_buf[j, pl.ds(y, 1)] = t_buf[j, pl.ds(y, 1)]

    def pair_copy(j):
        return remote(gp.at[j, :, 1 - c], cx.at[j], c2.at[0, j], c2.at[1, j], sibling)

    def group_stage(j):
        for o in range(1, NY):
            back_copy(o, j, yat(-o), yat(-o)).wait_recv()
        for q in range(CPC):
            rows = u_buf[j, :, q].reshape(NY * CAP2, DQ)
            sums = dot_tn(sel_buf[j * CPC + q], rows).astype(BF)
            gp[j, :, :, q] = sums.reshape(NZ, CORES, TD, DQ)
        start(pair_copy(j))

    def sum_copy(o, j, dst):
        return remote(q_buf.at[j, o], zb.at[j, o], z2.at[0, o, j], z2.at[1, o, j], at_z(dst))

    def pair_sum(j, zd):
        mine = gp[j, pl.ds(zd, 1), pl.ds(c, 1)].reshape(CPC, TD, DQ).astype(F32)
        return mine + cx[j, pl.ds(zd, 1)].reshape(CPC, TD, DQ).astype(F32)

    def pair_stage(j):
        pair_copy(j).wait_recv()
        for o in range(1, NZ):
            zd = zat(o)
            q_buf[j, o] = pair_sum(j, zd).astype(BF)
            start(sum_copy(o, j, zd))

    def sum_stage(j):
        total = pair_sum(j, z)
        for o in range(1, NZ):
            sum_copy(o, j, zat(-o)).wait_recv()
            total = total + zb[j, o].astype(F32)
        o_buf[j * CPC : (j + 1) * CPC] = total.astype(BF)

    stages = [gather_stage, pick_stage]
    stages += [functools.partial(rs_stage, k) for k in range(half_x)]
    stages += [act_stage]
    stages += [functools.partial(ag_stage, k) for k in range(1, half_x + 1)]
    stages += [group_stage, pair_stage, sum_stage]
    for t in range(len(stages) + NCH - 1):
        for j in range(NCH):
            if 0 <= t - j < len(stages):
                stages[t - j](j)

    for o in range(1, NX):
        xd = xat(o)
        start(remote(o_buf.at[xd], f_buf.at[x], x2.at[0, o], x2.at[1, o], at_x(xd)))
    f_buf[pl.ds(x, 1)] = o_buf[pl.ds(x, 1)]
    for o in range(1, NX):
        xs = xat(-o)
        remote(o_buf.at[xs], f_buf.at[xs], x2.at[0, o], x2.at[1, o], at_x(xs)).wait_recv()
    out[...] = jnp.concatenate([f_buf[d].astype(F32) for d in range(NX)], axis=1).astype(BF)
    for copy in sends:
        copy.wait_send()


def shards(tokens, gate_weight, up_weight, hidden_grad, expert_ids, expert_slot):
    NG = lax.axis_size("group")
    NY = EXP_GRP
    NX = lax.axis_size("ingroup") // NY
    NZ = NG // CORES
    TD, D = tokens.shape
    DQ = D // NX
    HQ = hidden_grad.shape[2]
    CAP = hidden_grad.shape[1]
    LANES = DQ + META
    half_x = NX // 2
    NCH = NX // CPC
    hbm = pl.BlockSpec(memory_space=pltpu.HBM)
    dma = pltpu.SemaphoreType.DMA
    return pl.pallas_call(
        functools.partial(kernel, (NX, NY, NZ)),
        out_shape=jax.ShapeDtypeStruct((TD, D), BF),
        in_specs=[hbm] * 6,
        out_specs=pl.BlockSpec(memory_space=pltpu.VMEM),
        scratch_shapes=[
            pltpu.VMEM(tokens.shape, BF),
            pltpu.VMEM(expert_ids.shape, jnp.int32),
            pltpu.VMEM(expert_slot.shape, jnp.int32),
            pltpu.VMEM((NX, TD, LANES), BF),
            pltpu.VMEM((NX, TD, LANES), BF),
            pltpu.VMEM((NX, NZ, CORES, TD, LANES), BF),
            pltpu.VMEM((NCH, NY, CPC, CAP2, DQ), BF),
            pltpu.VMEM((NCH, NY, CPC, CAP2, DQ), BF),
            pltpu.VMEM((NX, DQ, 2 * HQ), BF),
            pltpu.VMEM((CAP, HQ), BF),
            pltpu.VMEM((2, half_x, CAP, 2 * HQ), BF),
            pltpu.VMEM((2, half_x, CAP, 2 * HQ), BF),
            pltpu.VMEM((NX, CAP, 2 * HQ), BF),
            pltpu.VMEM((CAP, DQ), F32),
            pltpu.VMEM((NCH, NY, CPC, CAP2, DQ), BF),
            pltpu.VMEM((NCH, NY, CPC, CAP2, DQ), BF),
            pltpu.VMEM((NX, NY * CAP2, NG * TD), BF),
            pltpu.VMEM((NCH, NZ, CORES, CPC, TD, DQ), BF),
            pltpu.VMEM((NCH, NZ, CPC, TD, DQ), BF),
            pltpu.VMEM((NCH, NZ, CPC, TD, DQ), BF),
            pltpu.VMEM((NCH, NZ, CPC, TD, DQ), BF),
            pltpu.VMEM((NX, TD, DQ), BF),
            pltpu.VMEM((NX, TD, DQ), BF),
            dma((4,)),
            dma((NX * 2,)),
            dma((2, NX)),
            dma((2, NZ, NCH)),
            dma((2, NCH)),
            dma((2, NY, NCH)),
            dma((2, 2, half_x, NCH)),
            dma((2, 2, half_x, NCH)),
            dma((2, NY, NCH)),
            dma((2, NCH)),
            dma((2, NZ, NCH)),
            dma((2, NX)),
        ],
        compiler_params=pltpu.CompilerParams(
            collective_id=0, has_side_effects=True, vmem_limit_bytes=VMEM_BYTES
        ),
    )(tokens, expert_ids, expert_slot, gate_weight[0], up_weight[0], hidden_grad[0])


def solution(mesh):
    in_specs = (
        P(("group", "ingroup"), None),
        P(("group", "ingroup"), None, None),
        P(("group", "ingroup"), None, None),
        P(("group", "ingroup"), None, None),
        P(("group", "ingroup"), None),
        P(("group", "ingroup"), None),
    )
    out_specs = P(("group", "ingroup"), None)
    return jax.shard_map(shards, mesh=mesh, in_specs=in_specs, out_specs=out_specs, check_vma=False)
```

```python
import functools

import jax
import jax.numpy as jnp
from jax import lax
from jax.experimental import pallas as pl
from jax.experimental.pallas import tpu as pltpu
from jax.sharding import PartitionSpec as P

MESH = pl.DeviceIdType.MESH
BF = jnp.bfloat16
F32 = jnp.float32
CORES = 2
EXP_GRP = 8
CAP1 = 4
CAP2 = 8
META = 64
CHUNKS = (2, 2, 2, 2)
ORDER = (
    0, 0, 1, 0, 1, 0, 2, 0, 1, 2, 1, 0, 3, 2, 3, 1, 0, 2, 1, 3, 0, 2, 3, 1, 0, 2, 3, 1, 0, 2, 3,
    0, 1, 2, 3, 0, 1, 2, 0, 3, 1, 2, 3, 2, 0, 1, 3, 1, 3, 2, 2, 1, 3, 3, 2, 3,
)
VMEM_BYTES = 62 * 1024 * 1024


def remote(src, dst, send_sem, recv_sem, device):
    return pltpu.make_async_remote_copy(
        src_ref=src,
        dst_ref=dst,
        send_sem=send_sem,
        recv_sem=recv_sem,
        device_id=device,
        device_id_type=MESH,
    )


def dot_nt(a, b):
    return lax.dot_general(a, b, (((1,), (1,)), ((), ())), preferred_element_type=F32)


def dot_tn(a, b):
    return lax.dot_general(a, b, (((0,), (0,)), ((), ())), preferred_element_type=F32)


def kernel(
    dims,
    tokens,
    ids,
    slots,
    wg,
    wu,
    hg,
    out,
    tok_in,
    ids_in,
    slots_in,
    tok,
    a_buf,
    g_buf,
    s_buf,
    r_buf,
    w2,
    h_buf,
    rs_s,
    rs_r,
    ag,
    acc,
    t_buf,
    u_buf,
    sel_buf,
    gp,
    cx,
    q_buf,
    zb,
    o_buf,
    f_buf,
    in_sem,
    w_sem,
    x1,
    z1,
    c1,
    y1,
    rs_sem,
    ag_sem,
    y2,
    c2,
    z2,
    x2,
):
    NX, NY, NZ = dims
    NG = NZ * CORES
    TD = tok.shape[1]
    LANES = tok.shape[2]
    DQ = LANES - META
    HQ = hg.shape[1]
    RG = NX * CAP2
    CHUNK_ROWS = NY * CAP2
    NCH = len(CHUNKS)
    first = [sum(CHUNKS[:j]) for j in range(NCH)]
    assert sum(CHUNKS) == NX
    half_x = NX // 2

    g = lax.axis_index("group")
    p = lax.axis_index("ingroup")
    z, c = lax.div(g, CORES), lax.rem(g, CORES)
    y, x = lax.div(p, NX), lax.rem(p, NX)

    def xat(o):
        return lax.rem(x + (o + NX), NX)

    def yat(o):
        return lax.rem(y + (o + NY), NY)

    def zat(o):
        return lax.rem(z + (o + NZ), NZ)

    def at_x(xx):
        return (g, y * NX + xx)

    def at_y(yy):
        return (g, yy * NX + x)

    def at_z(zz):
        return (zz * CORES + c, p)

    sibling = (z * CORES + (1 - c), p)
    sends = []

    def start(copy):
        copy.start()
        sends.append(copy)

    inputs = [
        pltpu.make_async_copy(ids, ids_in, in_sem.at[0]),
        pltpu.make_async_copy(slots, slots_in, in_sem.at[1]),
        pltpu.make_async_copy(tokens, tok_in, in_sem.at[2]),
    ]
    for load in inputs:
        load.start()

    barrier = pltpu.get_barrier_semaphore()
    peers = [at_x(xat(o)) for o in range(1, NX)]
    peers += [at_y(yat(o)) for o in range(1, NY)]
    peers += [at_z(zat(o)) for o in range(1, NZ)]
    peers += [sibling]
    for peer in peers:
        pl.semaphore_signal(barrier, inc=1, device_id=peer, device_id_type=MESH)

    loads = []
    for d in range(NX):
        for n, w in enumerate((wg, wu)):
            loads.append(
                pltpu.make_async_copy(
                    w.at[:, pl.ds(d * HQ, HQ)],
                    w2.at[d, :, pl.ds(n * HQ, HQ)],
                    w_sem.at[d * 2 + n],
                )
            )
    loads.append(pltpu.make_async_copy(hg, h_buf, in_sem.at[3]))
    for load in loads:
        load.start()
    for load in inputs:
        load.wait()

    names, places = ids_in[...], slots_in[...]
    group_of = lax.div(names, EXP_GRP)
    lane = lax.broadcasted_iota(jnp.int32, (TD, 128), 1)
    named = jnp.zeros((TD, 128), F32)
    for k in range(names.shape[1]):
        named = jnp.where(group_of[:, k : k + 1] == lane, 1.0, named)
    before = lax.broadcasted_iota(jnp.int32, (TD, TD), 1) < lax.broadcasted_iota(jnp.int32, (TD, TD), 0)
    rank = jnp.dot(
        jnp.where(before, 1.0, 0.0).astype(BF), named.astype(BF), preferred_element_type=F32
    )
    fits = jnp.where(rank < CAP1, named, 0.0)
    meta = jnp.zeros((TD, 128), F32)
    for k in range(names.shape[1]):
        in_group = jnp.sum(jnp.where(group_of[:, k : k + 1] == lane, fits, 0.0), axis=1, keepdims=True)
        place = places[:, k : k + 1]
        name = jnp.where((in_group > 0.0) & (place >= 0), names[:, k : k + 1], 255).astype(F32)
        meta = jnp.where(lane == k, name, meta)
        meta = jnp.where(lane == 8 + k, jnp.maximum(place, 0).astype(F32), meta)
    features = tok_in[...].astype(F32)
    for d in range(NX):
        block = jnp.concatenate([features[:, d * DQ : (d + 1) * DQ], meta[:, :META]], axis=1)
        tok[d] = block.astype(BF)
    pl.semaphore_wait(barrier, len(peers))

    for o in range(1, NX):
        xd = xat(o)
        start(remote(tok.at[xd], a_buf.at[x], x1.at[0, o], x1.at[1, o], at_x(xd)))
    a_buf[pl.ds(x, 1)] = tok[pl.ds(x, 1)]
    for o in range(1, NX):
        xs = xat(-o)
        remote(tok.at[xs], a_buf.at[xs], x1.at[0, o], x1.at[1, o], at_x(xs)).wait_recv()

    def z_copy(o, j, src, dst):
        cols = pl.ds(first[j], CHUNKS[j])
        return remote(
            a_buf.at[cols], g_buf.at[cols, src, c], z1.at[0, o, j], z1.at[1, o, j], at_z(dst)
        )

    def z_send(j):
        for o in range(1, NZ):
            start(z_copy(o, j, z, zat(o)))

    z_send(0)
    g_buf[:, pl.ds(z, 1), pl.ds(c, 1)] = a_buf[...].reshape(NX, 1, 1, TD, LANES)

    def core_copy(j, core):
        part = g_buf.at[pl.ds(first[j], CHUNKS[j]), :, core]
        return remote(part, part, c1.at[0, j], c1.at[1, j], sibling)

    def gather_stage(j):
        for o in range(1, NZ):
            z_copy(o, j, zat(-o), zat(-o)).wait_recv()
        start(core_copy(j, c))
        if j + 1 < NCH:
            z_send(j + 1)

    pick_row = lax.broadcasted_iota(jnp.int32, (8, 128), 0)
    pick_lane = lax.broadcasted_iota(jnp.int32, (8, 128), 1) - (128 - META)
    pick = jnp.where(pick_lane == pick_row, 8.0, jnp.where(pick_lane == 8 + pick_row, 1.0, 0.0))
    pick = pick.astype(BF)
    code_of = lax.broadcasted_iota(jnp.int32, (NY * CAP2, NG * TD), 0) + g * (NY * CAP2)
    code_of = code_of.astype(F32)

    def blocks(j, row):
        return pl.ds(first[j] * NY + row * CHUNKS[j], CHUNKS[j])

    def y_copy(o, j, src, dst):
        return remote(
            s_buf.at[blocks(j, dst)], r_buf.at[blocks(j, src)], y1.at[0, o, j], y1.at[1, o, j], at_y(dst)
        )

    def pick_stage(j):
        core_copy(j, 1 - c).wait_recv()
        for q in range(CHUNKS[j]):
            xc = first[j] + q
            rows = g_buf[xc].reshape(NG * TD, LANES)
            codes = dot_nt(pick, rows[:, LANES - 128 :])
            sel = jnp.zeros(code_of.shape, F32)
            for k in range(8):
                sel = jnp.where(codes[k : k + 1, :] == code_of, 1.0, sel)
            sel = sel.astype(BF)
            sel_buf[xc] = sel
            picked = jnp.dot(sel, rows[:, :DQ], preferred_element_type=F32).astype(BF)
            for e in range(NY):
                s_buf[first[j] * NY + e * CHUNKS[j] + q] = picked[e * CAP2 : (e + 1) * CAP2]
        for o in range(1, NY):
            start(y_copy(o, j, y, yat(o)))
        r_buf[blocks(j, y)] = s_buf[blocks(j, y)]

    def weights(d):
        return w2[pl.ds(d, 1)].reshape(DQ, 2 * HQ)

    def span(j, half=None):
        base, size = first[j] * CHUNK_ROWS, CHUNKS[j] * CHUNK_ROWS
        if half is None:
            return pl.ds(base, size)
        return pl.ds(base + half * (size // 2), size // 2)

    def slot_rows(j):
        return r_buf[first[j] * NY : (first[j] + CHUNKS[j]) * NY].reshape(CHUNKS[j] * CHUNK_ROWS, DQ)

    def rs_copy(way, k, j):
        rows = span(j, None if k else way)
        return remote(
            rs_s.at[way, k, rows],
            rs_r.at[way, k, rows],
            rs_sem.at[0, way, k, j],
            rs_sem.at[1, way, k, j],
            at_x(xat(1 - 2 * way)),
        )

    def ag_copy(way, k, j, src):
        rows = span(j, None if k < half_x - 1 else way)
        return remote(
            ag.at[src, rows],
            ag.at[src, rows],
            ag_sem.at[0, way, k, j],
            ag_sem.at[1, way, k, j],
            at_x(xat(1 - 2 * way)),
        )

    def rs_stage(k, j):
        if k == 0:
            for o in range(1, NY):
                y_copy(o, j, yat(-o), yat(-o)).wait_recv()
            if j == 0:
                for load in loads:
                    load.wait()
        size = CHUNKS[j] * CHUNK_ROWS // 2
        lhs = slot_rows(j)
        for way in range(2):
            sign = 1 - 2 * way
            w = weights(xat(sign * (half_x - k)))
            mine = span(j, way)
            other = span(j, 1 - way)
            if k == 0:
                part = lhs[way * size : way * size + size]
                rs_s[way, 0, mine] = jnp.dot(part, w, preferred_element_type=F32).astype(BF)
            else:
                part = jnp.dot(lhs, w, preferred_element_type=F32)
                rs_copy(way, k - 1, j).wait_recv()
                if k == 1:
                    own = part[way * size : way * size + size]
                    rest = part[(1 - way) * size : (1 - way) * size + size]
                    rs_s[way, 1, mine] = (own + rs_r[way, 0, mine].astype(F32)).astype(BF)
                    rs_s[way, 1, other] = rest.astype(BF)
                else:
                    rows = span(j)
                    rs_s[way, k, rows] = (part + rs_r[way, k - 1, rows].astype(F32)).astype(BF)
            start(rs_copy(way, k, j))

    def act_stage(j):
        rows = span(j)
        pre = jnp.dot(slot_rows(j), weights(x), preferred_element_type=F32)
        for way in range(2):
            rs_copy(way, half_x - 1, j).wait_recv()
            pre = pre + rs_r[way, half_x - 1, rows].astype(F32)
        pre_gate, pre_up = pre[:, :HQ], pre[:, HQ:]
        hidden = jnp.concatenate(
            [
                h_buf[ys * RG + first[j] * CAP2 : ys * RG + (first[j] + CHUNKS[j]) * CAP2]
                for ys in range(NY)
            ],
            axis=0,
        ).astype(F32)
        sig = jax.nn.sigmoid(pre_gate)
        both = jnp.concatenate(
            [
                (hidden * pre_up * sig * (1.0 + pre_gate * (1.0 - sig))).astype(BF),
                (hidden * pre_gate * sig).astype(BF),
            ],
            axis=1,
        )
        ag[pl.ds(x, 1), rows] = both.reshape(1, CHUNKS[j] * CHUNK_ROWS, 2 * HQ)
        for way in range(2):
            start(ag_copy(way, 0, j, x))
        acc[rows] = dot_nt(both, weights(x))

    def back_copy(o, j, src, dst):
        return remote(
            t_buf.at[blocks(j, dst)], u_buf.at[blocks(j, src)], y2.at[0, o, j], y2.at[1, o, j], at_y(dst)
        )

    def ag_stage(k, j):
        rows = span(j)
        for way in range(2):
            sign = 1 - 2 * way
            src = xat(-sign * k)
            ag_copy(way, k - 1, j, src).wait_recv()
            if k < half_x:
                start(ag_copy(way, k, j, src))
        if k < half_x:
            total = acc[rows]
            for src in (xat(-k), xat(k)):
                block = ag[pl.ds(src, 1), rows].reshape(CHUNKS[j] * CHUNK_ROWS, 2 * HQ)
                total = total + dot_nt(block, weights(src))
            acc[rows] = total
        else:
            src = xat(half_x)
            block = ag[pl.ds(src, 1), rows].reshape(CHUNKS[j] * CHUNK_ROWS, 2 * HQ)
            total = acc[rows] + dot_nt(block, weights(src))
            t_buf[first[j] * NY : (first[j] + CHUNKS[j]) * NY] = total.astype(BF).reshape(-1, CAP2, DQ)
            for o in range(1, NY):
                start(back_copy(o, j, y, yat(o)))
            u_buf[blocks(j, y)] = t_buf[blocks(j, y)]

    def pair_copy(j):
        away = pl.ds((first[j] * CORES + (1 - c) * CHUNKS[j]) * NZ, CHUNKS[j] * NZ)
        return remote(gp.at[away], cx.at[pl.ds(first[j] * NZ, CHUNKS[j] * NZ)], c2.at[0, j], c2.at[1, j], sibling)

    def group_stage(j):
        for o in range(1, NY):
            back_copy(o, j, yat(-o), yat(-o)).wait_recv()
        n = CHUNKS[j]
        for q in range(n):
            rows = jnp.concatenate([u_buf[first[j] * NY + e * n + q] for e in range(NY)], axis=0)
            sums = dot_tn(sel_buf[first[j] + q], rows).astype(BF)
            for zz in range(NZ):
                for cc in range(CORES):
                    row = (zz * CORES + cc) * TD
                    gp[(first[j] * CORES + cc * n) * NZ + zz * n + q] = sums[row : row + TD]
        start(pair_copy(j))

    def sum_copy(o, j, dst):
        part = pl.ds(first[j] * NZ + o * CHUNKS[j], CHUNKS[j])
        return remote(q_buf.at[part], zb.at[part], z2.at[0, o, j], z2.at[1, o, j], at_z(dst))

    def pair_sum(j, zd):
        n = CHUNKS[j]
        mine = gp[pl.ds((first[j] * CORES + c * n) * NZ + zd * n, n)].astype(F32)
        return mine + cx[pl.ds(first[j] * NZ + zd * n, n)].astype(F32)

    def pair_stage(j):
        pair_copy(j).wait_recv()
        for o in range(1, NZ):
            zd = zat(o)
            q_buf[first[j] * NZ + o * CHUNKS[j] : first[j] * NZ + (o + 1) * CHUNKS[j]] = pair_sum(j, zd).astype(BF)
            start(sum_copy(o, j, zd))

    def sum_stage(j):
        total = pair_sum(j, z)
        for o in range(1, NZ):
            sum_copy(o, j, zat(-o)).wait_recv()
            total = total + zb[first[j] * NZ + o * CHUNKS[j] : first[j] * NZ + (o + 1) * CHUNKS[j]].astype(F32)
        o_buf[first[j] : first[j] + CHUNKS[j]] = total.astype(BF)

    stages = [gather_stage, pick_stage]
    stages += [functools.partial(rs_stage, k) for k in range(half_x)]
    stages += [act_stage]
    stages += [functools.partial(ag_stage, k) for k in range(1, half_x + 1)]
    stages += [group_stage, pair_stage, sum_stage]
    at = [iter(stages) for _ in range(NCH)]
    for j in ORDER:
        next(at[j])(j)

    for o in range(1, NX):
        xd = xat(o)
        start(remote(o_buf.at[xd], f_buf.at[x], x2.at[0, o], x2.at[1, o], at_x(xd)))
    f_buf[pl.ds(x, 1)] = o_buf[pl.ds(x, 1)]
    for o in range(1, NX):
        xs = xat(-o)
        remote(o_buf.at[xs], f_buf.at[xs], x2.at[0, o], x2.at[1, o], at_x(xs)).wait_recv()
    out[...] = jnp.concatenate([f_buf[d].astype(F32) for d in range(NX)], axis=1).astype(BF)
    for copy in sends:
        copy.wait_send()


def shards(tokens, gate_weight, up_weight, hidden_grad, expert_ids, expert_slot):
    NG = lax.axis_size("group")
    NY = EXP_GRP
    NX = lax.axis_size("ingroup") // NY
    NZ = NG // CORES
    TD, D = tokens.shape
    DQ = D // NX
    HQ = hidden_grad.shape[2]
    CAP = hidden_grad.shape[1]
    LANES = DQ + META
    half_x = NX // 2
    NCH = len(CHUNKS)
    hbm = pl.BlockSpec(memory_space=pltpu.HBM)
    dma = pltpu.SemaphoreType.DMA
    return pl.pallas_call(
        functools.partial(kernel, (NX, NY, NZ)),
        out_shape=jax.ShapeDtypeStruct((TD, D), BF),
        in_specs=[hbm] * 6,
        out_specs=pl.BlockSpec(memory_space=pltpu.VMEM),
        scratch_shapes=[
            pltpu.VMEM(tokens.shape, BF),
            pltpu.VMEM(expert_ids.shape, jnp.int32),
            pltpu.VMEM(expert_slot.shape, jnp.int32),
            pltpu.VMEM((NX, TD, LANES), BF),
            pltpu.VMEM((NX, TD, LANES), BF),
            pltpu.VMEM((NX, NZ, CORES, TD, LANES), BF),
            pltpu.VMEM((NX * NY, CAP2, DQ), BF),
            pltpu.VMEM((NX * NY, CAP2, DQ), BF),
            pltpu.VMEM((NX, DQ, 2 * HQ), BF),
            pltpu.VMEM((CAP, HQ), BF),
            pltpu.VMEM((2, half_x, CAP, 2 * HQ), BF),
            pltpu.VMEM((2, half_x, CAP, 2 * HQ), BF),
            pltpu.VMEM((NX, CAP, 2 * HQ), BF),
            pltpu.VMEM((CAP, DQ), F32),
            pltpu.VMEM((NX * NY, CAP2, DQ), BF),
            pltpu.VMEM((NX * NY, CAP2, DQ), BF),
            pltpu.VMEM((NX, NY * CAP2, NG * TD), BF),
            pltpu.VMEM((NX * NZ * CORES, TD, DQ), BF),
            pltpu.VMEM((NX * NZ, TD, DQ), BF),
            pltpu.VMEM((NX * NZ, TD, DQ), BF),
            pltpu.VMEM((NX * NZ, TD, DQ), BF),
            pltpu.VMEM((NX, TD, DQ), BF),
            pltpu.VMEM((NX, TD, DQ), BF),
            dma((4,)),
            dma((NX * 2,)),
            dma((2, NX)),
            dma((2, NZ, NCH)),
            dma((2, NCH)),
            dma((2, NY, NCH)),
            dma((2, 2, half_x, NCH)),
            dma((2, 2, half_x, NCH)),
            dma((2, NY, NCH)),
            dma((2, NCH)),
            dma((2, NZ, NCH)),
            dma((2, NX)),
        ],
        compiler_params=pltpu.CompilerParams(
            collective_id=0, has_side_effects=True, vmem_limit_bytes=VMEM_BYTES
        ),
    )(tokens, expert_ids, expert_slot, gate_weight[0], up_weight[0], hidden_grad[0])


def solution(mesh):
    in_specs = (
        P(("group", "ingroup"), None),
        P(("group", "ingroup"), None, None),
        P(("group", "ingroup"), None, None),
        P(("group", "ingroup"), None, None),
        P(("group", "ingroup"), None),
        P(("group", "ingroup"), None),
    )
    out_specs = P(("group", "ingroup"), None)
    return jax.shard_map(shards, mesh=mesh, in_specs=in_specs, out_specs=out_specs, check_vma=False)
```

```python
import functools

import jax
import jax.numpy as jnp
from jax import lax
from jax.experimental import pallas as pl
from jax.experimental.pallas import tpu as pltpu
from jax.sharding import PartitionSpec as P

MESH = pl.DeviceIdType.MESH
BF = jnp.bfloat16
F32 = jnp.float32
CORES = 2
EXP_GRP = 8
CAP1 = 4
CAP2 = 8
META = 64
CHUNKS = (2, 2, 2, 2)
AHEAD = 2
ORDER = (
    0, 1, 0, 1, 2, 3, 2, 0, 3, 1, 0, 1, 2, 0, 3, 1, 2, 3, 0, 1, 2, 3, 0, 1, 2, 3, 0, 1, 2, 3, 0,
    1, 2, 3, 0, 1, 2, 0, 3, 1, 2, 3, 2, 0, 3, 1, 0, 1, 2, 3, 2, 3, 0, 1, 2, 3,
)
VMEM_BYTES = 62 * 1024 * 1024


def remote(src, dst, send_sem, recv_sem, device):
    return pltpu.make_async_remote_copy(
        src_ref=src,
        dst_ref=dst,
        send_sem=send_sem,
        recv_sem=recv_sem,
        device_id=device,
        device_id_type=MESH,
    )


def dot_nt(a, b):
    return lax.dot_general(a, b, (((1,), (1,)), ((), ())), preferred_element_type=F32)


def dot_tn(a, b):
    return lax.dot_general(a, b, (((0,), (0,)), ((), ())), preferred_element_type=F32)


def kernel(
    dims,
    tokens,
    ids,
    slots,
    wg,
    wu,
    hg,
    out,
    tok_in,
    ids_in,
    slots_in,
    tok,
    a_buf,
    g_buf,
    s_buf,
    r_buf,
    w2,
    h_buf,
    rs_s,
    rs_r,
    ag,
    acc,
    t_buf,
    u_buf,
    sel_buf,
    gp,
    cx,
    q_buf,
    zb,
    o_buf,
    f_buf,
    in_sem,
    w_sem,
    x1,
    z1,
    c1,
    y1,
    rs_sem,
    ag_sem,
    y2,
    c2,
    z2,
    x2,
):
    NX, NY, NZ = dims
    NG = NZ * CORES
    TD = tok.shape[1]
    LANES = tok.shape[2]
    DQ = LANES - META
    HQ = hg.shape[1]
    RG = NX * CAP2
    CHUNK_ROWS = NY * CAP2
    NCH = len(CHUNKS)
    first = [sum(CHUNKS[:j]) for j in range(NCH)]
    assert sum(CHUNKS) == NX
    half_x = NX // 2

    g = lax.axis_index("group")
    p = lax.axis_index("ingroup")
    z, c = lax.div(g, CORES), lax.rem(g, CORES)
    y, x = lax.div(p, NX), lax.rem(p, NX)

    def xat(o):
        return lax.rem(x + (o + NX), NX)

    def yat(o):
        return lax.rem(y + (o + NY), NY)

    def zat(o):
        return lax.rem(z + (o + NZ), NZ)

    def at_x(xx):
        return (g, y * NX + xx)

    def at_y(yy):
        return (g, yy * NX + x)

    def at_z(zz):
        return (zz * CORES + c, p)

    sibling = (z * CORES + (1 - c), p)
    sends = []

    def start(copy):
        copy.start()
        sends.append(copy)

    inputs = [
        pltpu.make_async_copy(ids, ids_in, in_sem.at[0]),
        pltpu.make_async_copy(slots, slots_in, in_sem.at[1]),
        pltpu.make_async_copy(tokens, tok_in, in_sem.at[2]),
    ]
    for load in inputs:
        load.start()

    barrier = pltpu.get_barrier_semaphore()
    peers = [at_x(xat(o)) for o in range(1, NX)]
    peers += [at_y(yat(o)) for o in range(1, NY)]
    peers += [at_z(zat(o)) for o in range(1, NZ)]
    peers += [sibling]
    for peer in peers:
        pl.semaphore_signal(barrier, inc=1, device_id=peer, device_id_type=MESH)

    loads = []
    for d in range(NX):
        for n, w in enumerate((wg, wu)):
            loads.append(
                pltpu.make_async_copy(
                    w.at[:, pl.ds(d * HQ, HQ)],
                    w2.at[d, :, pl.ds(n * HQ, HQ)],
                    w_sem.at[d * 2 + n],
                )
            )
    loads.append(pltpu.make_async_copy(hg, h_buf, in_sem.at[3]))
    for load in loads:
        load.start()
    for load in inputs:
        load.wait()

    names, places = ids_in[...], slots_in[...]
    group_of = lax.div(names, EXP_GRP)
    lane = lax.broadcasted_iota(jnp.int32, (TD, 128), 1)
    named = jnp.zeros((TD, 128), F32)
    for k in range(names.shape[1]):
        named = jnp.where(group_of[:, k : k + 1] == lane, 1.0, named)
    before = lax.broadcasted_iota(jnp.int32, (TD, TD), 1) < lax.broadcasted_iota(jnp.int32, (TD, TD), 0)
    rank = jnp.dot(
        jnp.where(before, 1.0, 0.0).astype(BF), named.astype(BF), preferred_element_type=F32
    )
    fits = jnp.where(rank < CAP1, named, 0.0)
    meta = jnp.zeros((TD, 128), F32)
    for k in range(names.shape[1]):
        in_group = jnp.sum(jnp.where(group_of[:, k : k + 1] == lane, fits, 0.0), axis=1, keepdims=True)
        place = places[:, k : k + 1]
        name = jnp.where((in_group > 0.0) & (place >= 0), names[:, k : k + 1], 255).astype(F32)
        meta = jnp.where(lane == k, name, meta)
        meta = jnp.where(lane == 8 + k, jnp.maximum(place, 0).astype(F32), meta)
    features = tok_in[...].astype(F32)
    for d in range(NX):
        block = jnp.concatenate([features[:, d * DQ : (d + 1) * DQ], meta[:, :META]], axis=1)
        tok[d] = block.astype(BF)
    pl.semaphore_wait(barrier, len(peers))

    for o in range(1, NX):
        xd = xat(o)
        start(remote(tok.at[xd], a_buf.at[x], x1.at[0, o], x1.at[1, o], at_x(xd)))
    a_buf[pl.ds(x, 1)] = tok[pl.ds(x, 1)]
    for o in range(1, NX):
        xs = xat(-o)
        remote(tok.at[xs], a_buf.at[xs], x1.at[0, o], x1.at[1, o], at_x(xs)).wait_recv()

    def z_copy(o, j, src, dst):
        cols = pl.ds(first[j], CHUNKS[j])
        return remote(
            a_buf.at[cols], g_buf.at[cols, src, c], z1.at[0, o, j], z1.at[1, o, j], at_z(dst)
        )

    def z_send(j):
        for o in range(1, NZ):
            start(z_copy(o, j, z, zat(o)))

    for j in range(AHEAD):
        z_send(j)
    g_buf[:, pl.ds(z, 1), pl.ds(c, 1)] = a_buf[...].reshape(NX, 1, 1, TD, LANES)

    def core_copy(j, core):
        part = g_buf.at[pl.ds(first[j], CHUNKS[j]), :, core]
        return remote(part, part, c1.at[0, j], c1.at[1, j], sibling)

    def gather_stage(j):
        for o in range(1, NZ):
            z_copy(o, j, zat(-o), zat(-o)).wait_recv()
        start(core_copy(j, c))
        if j + AHEAD < NCH:
            z_send(j + AHEAD)

    pick_row = lax.broadcasted_iota(jnp.int32, (8, 128), 0)
    pick_lane = lax.broadcasted_iota(jnp.int32, (8, 128), 1) - (128 - META)
    pick = jnp.where(pick_lane == pick_row, 8.0, jnp.where(pick_lane == 8 + pick_row, 1.0, 0.0))
    pick = pick.astype(BF)
    code_of = lax.broadcasted_iota(jnp.int32, (NY * CAP2, NG * TD), 0) + g * (NY * CAP2)
    code_of = code_of.astype(F32)

    def blocks(j, row):
        return pl.ds(first[j] * NY + row * CHUNKS[j], CHUNKS[j])

    def y_copy(o, j, src, dst):
        return remote(
            s_buf.at[blocks(j, dst)], r_buf.at[blocks(j, src)], y1.at[0, o, j], y1.at[1, o, j], at_y(dst)
        )

    def pick_stage(j):
        core_copy(j, 1 - c).wait_recv()
        for q in range(CHUNKS[j]):
            xc = first[j] + q
            rows = g_buf[xc].reshape(NG * TD, LANES)
            codes = dot_nt(pick, rows[:, LANES - 128 :])
            sel = jnp.zeros(code_of.shape, F32)
            for k in range(8):
                sel = jnp.where(codes[k : k + 1, :] == code_of, 1.0, sel)
            sel = sel.astype(BF)
            sel_buf[xc] = sel
            picked = jnp.dot(sel, rows[:, :DQ], preferred_element_type=F32).astype(BF)
            for e in range(NY):
                s_buf[first[j] * NY + e * CHUNKS[j] + q] = picked[e * CAP2 : (e + 1) * CAP2]
        for o in range(1, NY):
            start(y_copy(o, j, y, yat(o)))
        r_buf[blocks(j, y)] = s_buf[blocks(j, y)]

    def weights(d):
        return w2[pl.ds(d, 1)].reshape(DQ, 2 * HQ)

    def span(j, half=None):
        base, size = first[j] * CHUNK_ROWS, CHUNKS[j] * CHUNK_ROWS
        if half is None:
            return pl.ds(base, size)
        return pl.ds(base + half * (size // 2), size // 2)

    def slot_rows(j):
        return r_buf[first[j] * NY : (first[j] + CHUNKS[j]) * NY].reshape(CHUNKS[j] * CHUNK_ROWS, DQ)

    def rs_copy(way, k, j):
        rows = span(j, None if k else way)
        return remote(
            rs_s.at[way, k, rows],
            rs_r.at[way, k, rows],
            rs_sem.at[0, way, k, j],
            rs_sem.at[1, way, k, j],
            at_x(xat(1 - 2 * way)),
        )

    def ag_copy(way, k, j, src):
        rows = span(j, None if k < half_x - 1 else way)
        return remote(
            ag.at[src, rows],
            ag.at[src, rows],
            ag_sem.at[0, way, k, j],
            ag_sem.at[1, way, k, j],
            at_x(xat(1 - 2 * way)),
        )

    def rs_stage(k, j):
        if k == 0:
            for o in range(1, NY):
                y_copy(o, j, yat(-o), yat(-o)).wait_recv()
            if j == 0:
                for load in loads:
                    load.wait()
        size = CHUNKS[j] * CHUNK_ROWS // 2
        lhs = slot_rows(j)
        for way in range(2):
            sign = 1 - 2 * way
            w = weights(xat(sign * (half_x - k)))
            mine = span(j, way)
            other = span(j, 1 - way)
            if k == 0:
                part = lhs[way * size : way * size + size]
                rs_s[way, 0, mine] = jnp.dot(part, w, preferred_element_type=F32).astype(BF)
            else:
                part = jnp.dot(lhs, w, preferred_element_type=F32)
                rs_copy(way, k - 1, j).wait_recv()
                if k == 1:
                    own = part[way * size : way * size + size]
                    rest = part[(1 - way) * size : (1 - way) * size + size]
                    rs_s[way, 1, mine] = (own + rs_r[way, 0, mine].astype(F32)).astype(BF)
                    rs_s[way, 1, other] = rest.astype(BF)
                else:
                    rows = span(j)
                    rs_s[way, k, rows] = (part + rs_r[way, k - 1, rows].astype(F32)).astype(BF)
            start(rs_copy(way, k, j))

    def act_stage(j):
        rows = span(j)
        pre = jnp.dot(slot_rows(j), weights(x), preferred_element_type=F32)
        for way in range(2):
            rs_copy(way, half_x - 1, j).wait_recv()
            pre = pre + rs_r[way, half_x - 1, rows].astype(F32)
        pre_gate, pre_up = pre[:, :HQ], pre[:, HQ:]
        hidden = jnp.concatenate(
            [
                h_buf[ys * RG + first[j] * CAP2 : ys * RG + (first[j] + CHUNKS[j]) * CAP2]
                for ys in range(NY)
            ],
            axis=0,
        ).astype(F32)
        sig = jax.nn.sigmoid(pre_gate)
        both = jnp.concatenate(
            [
                (hidden * pre_up * sig * (1.0 + pre_gate * (1.0 - sig))).astype(BF),
                (hidden * pre_gate * sig).astype(BF),
            ],
            axis=1,
        )
        ag[pl.ds(x, 1), rows] = both.reshape(1, CHUNKS[j] * CHUNK_ROWS, 2 * HQ)
        for way in range(2):
            start(ag_copy(way, 0, j, x))
        acc[rows] = dot_nt(both, weights(x))

    def back_copy(o, j, src, dst):
        return remote(
            t_buf.at[blocks(j, dst)], u_buf.at[blocks(j, src)], y2.at[0, o, j], y2.at[1, o, j], at_y(dst)
        )

    def ag_stage(k, j):
        rows = span(j)
        for way in range(2):
            sign = 1 - 2 * way
            src = xat(-sign * k)
            ag_copy(way, k - 1, j, src).wait_recv()
            if k < half_x:
                start(ag_copy(way, k, j, src))
        if k < half_x:
            total = acc[rows]
            for src in (xat(-k), xat(k)):
                block = ag[pl.ds(src, 1), rows].reshape(CHUNKS[j] * CHUNK_ROWS, 2 * HQ)
                total = total + dot_nt(block, weights(src))
            acc[rows] = total
        else:
            src = xat(half_x)
            block = ag[pl.ds(src, 1), rows].reshape(CHUNKS[j] * CHUNK_ROWS, 2 * HQ)
            total = acc[rows] + dot_nt(block, weights(src))
            t_buf[first[j] * NY : (first[j] + CHUNKS[j]) * NY] = total.astype(BF).reshape(-1, CAP2, DQ)
            for o in range(1, NY):
                start(back_copy(o, j, y, yat(o)))
            u_buf[blocks(j, y)] = t_buf[blocks(j, y)]

    def pair_copy(j):
        away = pl.ds((first[j] * CORES + (1 - c) * CHUNKS[j]) * NZ, CHUNKS[j] * NZ)
        return remote(gp.at[away], cx.at[pl.ds(first[j] * NZ, CHUNKS[j] * NZ)], c2.at[0, j], c2.at[1, j], sibling)

    def group_stage(j):
        for o in range(1, NY):
            back_copy(o, j, yat(-o), yat(-o)).wait_recv()
        n = CHUNKS[j]
        for q in range(n):
            rows = jnp.concatenate([u_buf[first[j] * NY + e * n + q] for e in range(NY)], axis=0)
            sums = dot_tn(sel_buf[first[j] + q], rows).astype(BF)
            for zz in range(NZ):
                for cc in range(CORES):
                    row = (zz * CORES + cc) * TD
                    gp[(first[j] * CORES + cc * n) * NZ + zz * n + q] = sums[row : row + TD]
        start(pair_copy(j))

    def sum_copy(o, j, dst):
        part = pl.ds(first[j] * NZ + o * CHUNKS[j], CHUNKS[j])
        return remote(q_buf.at[part], zb.at[part], z2.at[0, o, j], z2.at[1, o, j], at_z(dst))

    def pair_sum(j, zd):
        n = CHUNKS[j]
        mine = gp[pl.ds((first[j] * CORES + c * n) * NZ + zd * n, n)].astype(F32)
        return mine + cx[pl.ds(first[j] * NZ + zd * n, n)].astype(F32)

    def pair_stage(j):
        pair_copy(j).wait_recv()
        for o in range(1, NZ):
            zd = zat(o)
            q_buf[first[j] * NZ + o * CHUNKS[j] : first[j] * NZ + (o + 1) * CHUNKS[j]] = pair_sum(j, zd).astype(BF)
            start(sum_copy(o, j, zd))

    def out_copy(dst, src):
        return remote(o_buf.at[dst], f_buf.at[src], x2.at[0, dst], x2.at[1, src], at_x(dst))

    def sum_stage(j):
        total = pair_sum(j, z)
        for o in range(1, NZ):
            sum_copy(o, j, zat(-o)).wait_recv()
            total = total + zb[first[j] * NZ + o * CHUNKS[j] : first[j] * NZ + (o + 1) * CHUNKS[j]].astype(F32)
        o_buf[first[j] : first[j] + CHUNKS[j]] = total.astype(BF)
        for col in range(first[j], first[j] + CHUNKS[j]):

            @pl.when(x != col)
            def _():
                out_copy(col, x).start()

    stages = [gather_stage, pick_stage]
    stages += [functools.partial(rs_stage, k) for k in range(half_x)]
    stages += [act_stage]
    stages += [functools.partial(ag_stage, k) for k in range(1, half_x + 1)]
    stages += [group_stage, pair_stage, sum_stage]
    at = [iter(stages) for _ in range(NCH)]
    for j in ORDER:
        next(at[j])(j)

    f_buf[pl.ds(x, 1)] = o_buf[pl.ds(x, 1)]
    for o in range(1, NX):
        out_copy(xat(-o), xat(-o)).wait_recv()
        out_copy(xat(o), x).wait_send()
    out[...] = jnp.concatenate([f_buf[d].astype(F32) for d in range(NX)], axis=1).astype(BF)
    for copy in sends:
        copy.wait_send()


def shards(tokens, gate_weight, up_weight, hidden_grad, expert_ids, expert_slot):
    NG = lax.axis_size("group")
    NY = EXP_GRP
    NX = lax.axis_size("ingroup") // NY
    NZ = NG // CORES
    TD, D = tokens.shape
    DQ = D // NX
    HQ = hidden_grad.shape[2]
    CAP = hidden_grad.shape[1]
    LANES = DQ + META
    half_x = NX // 2
    NCH = len(CHUNKS)
    hbm = pl.BlockSpec(memory_space=pltpu.HBM)
    dma = pltpu.SemaphoreType.DMA
    return pl.pallas_call(
        functools.partial(kernel, (NX, NY, NZ)),
        out_shape=jax.ShapeDtypeStruct((TD, D), BF),
        in_specs=[hbm] * 6,
        out_specs=pl.BlockSpec(memory_space=pltpu.VMEM),
        scratch_shapes=[
            pltpu.VMEM(tokens.shape, BF),
            pltpu.VMEM(expert_ids.shape, jnp.int32),
            pltpu.VMEM(expert_slot.shape, jnp.int32),
            pltpu.VMEM((NX, TD, LANES), BF),
            pltpu.VMEM((NX, TD, LANES), BF),
            pltpu.VMEM((NX, NZ, CORES, TD, LANES), BF),
            pltpu.VMEM((NX * NY, CAP2, DQ), BF),
            pltpu.VMEM((NX * NY, CAP2, DQ), BF),
            pltpu.VMEM((NX, DQ, 2 * HQ), BF),
            pltpu.VMEM((CAP, HQ), BF),
            pltpu.VMEM((2, half_x, CAP, 2 * HQ), BF),
            pltpu.VMEM((2, half_x, CAP, 2 * HQ), BF),
            pltpu.VMEM((NX, CAP, 2 * HQ), BF),
            pltpu.VMEM((CAP, DQ), F32),
            pltpu.VMEM((NX * NY, CAP2, DQ), BF),
            pltpu.VMEM((NX * NY, CAP2, DQ), BF),
            pltpu.VMEM((NX, NY * CAP2, NG * TD), BF),
            pltpu.VMEM((NX * NZ * CORES, TD, DQ), BF),
            pltpu.VMEM((NX * NZ, TD, DQ), BF),
            pltpu.VMEM((NX * NZ, TD, DQ), BF),
            pltpu.VMEM((NX * NZ, TD, DQ), BF),
            pltpu.VMEM((NX, TD, DQ), BF),
            pltpu.VMEM((NX, TD, DQ), BF),
            dma((4,)),
            dma((NX * 2,)),
            dma((2, NX)),
            dma((2, NZ, NCH)),
            dma((2, NCH)),
            dma((2, NY, NCH)),
            dma((2, 2, half_x, NCH)),
            dma((2, 2, half_x, NCH)),
            dma((2, NY, NCH)),
            dma((2, NCH)),
            dma((2, NZ, NCH)),
            dma((2, NX)),
        ],
        compiler_params=pltpu.CompilerParams(
            collective_id=0, has_side_effects=True, vmem_limit_bytes=VMEM_BYTES
        ),
    )(tokens, expert_ids, expert_slot, gate_weight[0], up_weight[0], hidden_grad[0])


def solution(mesh):
    in_specs = (
        P(("group", "ingroup"), None),
        P(("group", "ingroup"), None, None),
        P(("group", "ingroup"), None, None),
        P(("group", "ingroup"), None, None),
        P(("group", "ingroup"), None),
        P(("group", "ingroup"), None),
    )
    out_specs = P(("group", "ingroup"), None)
    return jax.shard_map(shards, mesh=mesh, in_specs=in_specs, out_specs=out_specs, check_vma=False)
```
